32 devices in a mesh: groups: 2 (over y), expert: 4 (over x, core), dp: 4 (over z).
Axes of the slice: x: 2, y: 2, z: 4, core: 2. Of those that a mesh axis runs over, the one named last changes fastest.
Arguments:
- tokens: bfloat16 [2048, 7168], P(('groups', 'expert', 'dp')), parts along dimension 0, may hold values from -6 to 6
- expert_ids: int32 [2048, 8], P(('groups', 'expert', 'dp')), parts along dimension 0, may hold values from 0 to 255, all different within a row; in each aligned block of 64 rows (0 to 63, 64 to 127, ...) at most 4 rows name the same one
- gate_weights: float32 [2048, 8], P(('groups', 'expert', 'dp')), parts along dimension 0, may hold values from 0.05 to 0.6
- w_gate: bfloat16 [4, 7168, 2048], P('expert', None, 'dp'), may hold values from -0.0625 to 0.0625
- w_up: bfloat16 [4, 7168, 2048], P('expert', None, 'dp'), may hold values from -0.0625 to 0.0625
- w_down: bfloat16 [4, 2048, 7168], P('expert', 'dp'), may hold values from -0.125 to 0.125
Outputs:
- embedding: bfloat16 [2048, 7168], P(('groups', 'expert', 'dp')), parts along dimension 0
The draws below stay inside these ranges and needn't reach their ends.
There are 2 independent parts, one for each index of `groups`. The reference program is written for one: setup_inputs(seed, part) draws one part's arguments, and reference() takes and returns one part's arrays. A program takes and returns all parts, laid end to end along the dimension named above; an argument that names none is the same for every part. Nothing has to cross between parts.
Inputs may be any that keep to these rules, and one draw needn't show every extreme that they name: `expert_ids`: each token names 8 different experts; among the 64 tokens of one device no expert is named more than 4 times, a bound that some block reaches.
All inputs are finite; a program needn't handle non-finite values.
Results may differ from the reference program's by a relative error of at most 0.012.
Values may be sent and summed in bfloat16 or wider, within the bound.
No kernel may reach another device: no remote copies, remote signals or barrier semaphores. Data moves between devices by JAX's collectives and lax.ppermute only.
A program may use at most 64 MiB of HBM per device.

```python
import math
import jax
import jax.numpy as jnp
import numpy as np
from jax import lax

D = 7168
FF = 2048
EXPERTS = 256
TOPK = 8
CAP = 4
TOK_DEV = 64
EXP_WIN = 4
FF_DEV = 512
TOKENS = 1024
N_EXPERT = 4
N_DP = 4


def block_scale(rng, dims, cuts, low, high):
    factor_of, own = 1.0, jax.random.fold_in(rng, 6)
    for axis_at, shards_of in cuts:
        steps = jnp.exp(jax.random.uniform(jax.random.fold_in(own, axis_at), (shards_of,), jnp.float32, low / len(cuts), high / len(cuts)))
        factor_of = factor_of * jnp.repeat(steps, dims[axis_at] // shards_of).reshape([-1 if axis == axis_at else 1 for axis in range(len(dims))])
    return factor_of


def assign_block(own_key, own, number, rows, count, top, limit, skew):
    ranking = jax.random.permutation(own_key, count)
    packed, ordinary = shares(count, rows * top, limit, skew, True), shares(count, rows * top, limit, skew, False)
    places = jnp.arange(count)

    def named(sizes, rotation):
        used = int((sizes > 0).sum())
        fixed = max(1, used // 4)
        shifted = fixed + (places - fixed + rotation * (used - fixed)) % max(1, count - fixed)
        return jnp.zeros((count,), jnp.int32).at[ranking[jnp.where(places < fixed, places, shifted)]].set(jnp.asarray(sizes, jnp.int32))

    sizes = jnp.where(number % 4 == 0, named(packed, number // 4), named(ordinary, number - number // 4 - 1))
    mixed = jax.random.permutation(jax.random.fold_in(own, 3), count)
    giver, receiver = mixed[0:count // 2 * 2:2], mixed[1:count // 2 * 2:2]
    room = jnp.minimum(sizes[giver] - 1, limit - sizes[receiver]) // 2
    room = jnp.where((giver == ranking[0]) | (receiver == ranking[0]) | (sizes[receiver] == 0), 0, jnp.maximum(room, 0))
    shifted = jax.random.randint(jax.random.fold_in(own, 4), (count // 2,), 0, 1 << 20) % (room + 1)
    sizes = sizes.at[giver].add(-shifted).at[receiver].add(shifted)
    members = jnp.searchsorted(jnp.cumsum(sizes), jnp.arange(rows * top), side="right").astype(jnp.int32)
    table = members.reshape(top, rows).T
    table = table[jax.random.permutation(jax.random.fold_in(own, 1), rows)]
    rotation = jax.random.randint(jax.random.fold_in(own, 2), (rows, 1), 0, top)
    return jnp.take_along_axis(table, (jnp.arange(top)[None, :] + rotation) % top, axis=1)


def shares(number_of, total, bound, skew, full):
    loads = [(1 << 20) // math.isqrt(rank ** skew) + 1 for rank in range(1, number_of + 1)]
    largest = bound if full else min(bound, max(-(-total // number_of), total * loads[0] // sum(loads)))
    least = 1 if total - largest >= number_of - 1 else 0
    holding, rest = [largest] + [least] * (number_of - 1), total - largest - least * (number_of - 1)
    while rest > 0:
        free = [i for i in range(1, number_of) if holding[i] < largest] or [i for i in range(1, number_of) if holding[i] < bound]
        whole, remaining = sum([loads[i] for i in free]), rest
        for i in free:
            extra = min(bound - holding[i], max(1, remaining * loads[i] // whole), rest)
            holding[i] = holding[i] + extra
            rest = rest - extra
    return np.array(holding)


def centred(stream_key, shape, spread, limit, split=(), kind=jnp.bfloat16):
    drawn = jax.random.normal(stream_key, shape, jnp.float32) * spread
    if len(split) > 0:
        drawn = block_scale(stream_key, shape, split, -0.22, 0.18) * drawn
    return jnp.clip(drawn, min=-limit, max=limit).astype(kind)


def setup_inputs(seed: int = 0, part: int = 0) -> dict:
    seeds = jax.random.split(jax.random.key(seed), 7)
    part_keys = jax.random.split(jax.random.fold_in(seeds[6], part), 7)
    tokens = centred(part_keys[0], (TOKENS, D), 1.0, 6.0, ((0, 16),))
    expert_ids_keys = jax.random.split(jax.random.fold_in(part_keys[1], 1), TOKENS // TOK_DEV)
    expert_ids_turns = jax.random.permutation(jax.random.fold_in(part_keys[1], 3), TOKENS // TOK_DEV)
    expert_ids = jax.vmap(lambda own, number: assign_block(jax.random.fold_in(part_keys[1], 2), own, number, TOK_DEV, EXPERTS, TOPK, CAP, 2))(expert_ids_keys, expert_ids_turns).reshape((TOKENS, TOPK))
    gate_weights = jnp.clip(0.05 + 0.55 * jax.random.uniform(part_keys[2], (TOKENS, TOPK), jnp.float32) ** block_scale(part_keys[2], (TOKENS, TOPK), ((0, 16),), -0.2, 0.2), 0.05, 0.6)
    w_gate = centred(seeds[3], (EXP_WIN, D, FF), D ** -0.5, 0.0625, ((0, 4), (2, 4)))
    w_up = centred(seeds[4], (EXP_WIN, D, FF), D ** -0.5, 0.0625, ((0, 4), (2, 4)))
    w_down = centred(seeds[5], (EXP_WIN, FF, D), FF ** -0.5, 0.125, ((0, 4), (1, 4)))
    return {"tokens": tokens, "expert_ids": expert_ids, "gate_weights": gate_weights, "w_gate": w_gate, "w_up": w_up, "w_down": w_down}


def reference(tokens, expert_ids, gate_weights, w_gate, w_up, w_down):
    devices = N_EXPERT * N_DP
    by_device = tokens.reshape(devices, TOK_DEV, D).astype(jnp.float32)
    routing = expert_ids.reshape(devices, TOK_DEV, TOPK)
    gate_vals = gate_weights.reshape(devices, TOK_DEV, TOPK)
    slot_index = jnp.arange(CAP, dtype=jnp.int32)

    def one_expert(totals, expert_item):
        expert, gate_mat, up_mat, down_mat = expert_item
        matches = routing == expert
        chosen = jnp.sum(matches.astype(jnp.int32), axis=2)
        route_weight = jnp.sum(jnp.where(matches, gate_vals, jnp.float32(0.0)), axis=2)
        position = jnp.cumsum(chosen, axis=1) - chosen
        select = ((position[:, None, :] == slot_index[None, :, None]) & (chosen[:, None, :] > 0)).astype(jnp.float32)
        row_block = jnp.einsum("pct,ptd->pcd", select, by_device, precision=lax.Precision.HIGHEST)
        row_block = row_block.astype(jnp.bfloat16).reshape(devices * CAP, D)
        gate_proj = jnp.dot(row_block, gate_mat, preferred_element_type=jnp.float32)
        up_proj = jnp.dot(row_block, up_mat, preferred_element_type=jnp.float32)
        hidden = (jax.nn.silu(gate_proj) * up_proj).astype(jnp.bfloat16)
        summed = jnp.zeros((devices * CAP, D), jnp.float32)
        for shard_index in range(FF // FF_DEV):
            lower_unit = shard_index * FF_DEV
            partial_value = jnp.dot(hidden[:, lower_unit:lower_unit + FF_DEV], down_mat[lower_unit:lower_unit + FF_DEV], preferred_element_type=jnp.float32)
            partial_value = lax.optimization_barrier(partial_value.astype(jnp.bfloat16))
            summed = summed + partial_value.astype(jnp.float32)
        expert_out = summed.reshape(devices, CAP, D)
        combine = select * route_weight[:, None, :]
        totals = totals + jnp.einsum("pct,pcd->ptd", combine, expert_out, precision=lax.Precision.HIGHEST)
        return totals, None

    start_totals = jnp.zeros((devices, TOK_DEV, D), jnp.float32)
    expert_list = jnp.arange(EXP_WIN, dtype=jnp.int32)
    totals, unused = lax.scan(one_expert, start_totals, (expert_list, w_gate, w_up, w_down))
    return totals.reshape(TOKENS, D).astype(jnp.bfloat16)
```

```python
import jax
import jax.numpy as jnp
from jax import lax
from jax.sharding import PartitionSpec as P

CAP = 4
CORES = 2


def routing(expert_ids, gate_weights, experts):
    matches = expert_ids[:, :, None] == experts[None, None, :]
    chosen = jnp.any(matches, axis=1)
    weight = jnp.sum(jnp.where(matches, gate_weights[:, :, None], jnp.float32(0.0)), axis=1)
    count = chosen.astype(jnp.int32)
    tokens = count.shape[0]
    before = lax.broadcasted_iota(jnp.int32, (tokens, tokens), 0) > lax.broadcasted_iota(jnp.int32, (tokens, tokens), 1)
    position = jnp.dot(
        before.astype(jnp.bfloat16), count.astype(jnp.bfloat16), preferred_element_type=jnp.float32
    ).astype(jnp.int32)
    slot = jnp.arange(CAP, dtype=jnp.int32)
    select = (position.T[:, None, :] == slot[None, :, None]) & chosen.T[:, None, :]
    return select, weight


def ring(n):
    return [(i, (i + 1) % n) for i in range(n)]


def gather_ring(block, n):
    parts = [block]
    for _ in range(n - 1):
        parts.append(lax.ppermute(parts[-1], "dp", ring(n)))
    return parts


def scatter_ring(parts, n):
    total = parts[1 % n]
    for step in range(1, n):
        arrived = lax.ppermute(total, "dp", ring(n))
        total = (arrived.astype(jnp.float32) + parts[(step + 1) % n].astype(jnp.float32)).astype(jnp.bfloat16)
    return total


def local(tokens, expert_ids, gate_weights, w_gate, w_up, w_down):
    window = lax.axis_size("expert")
    shards = lax.axis_size("dp")
    chips = window // CORES
    width = tokens.shape[1]
    me = lax.axis_index("expert")
    chip, core = me // CORES, me % CORES
    offset = jnp.arange(window, dtype=jnp.int32)
    core_offset, chip_offset = offset // chips, offset % chips
    experts = ((chip + chip_offset) % chips) * CORES + (core + core_offset) % CORES
    select, route_weight = routing(expert_ids, gate_weights, experts)
    flat_select = select.reshape(window * CAP, -1)
    outgoing = jnp.dot(
        flat_select.astype(jnp.bfloat16), tokens, preferred_element_type=jnp.float32
    ).astype(jnp.bfloat16)

    core_pairs = [(i, i ^ 1) for i in range(window)]

    def chip_pairs(shift):
        return [
            (c * CORES + k, ((c + shift) % chips) * CORES + k) for c in range(chips) for k in range(CORES)
        ]

    half = chips * CAP
    kept = outgoing[:half].reshape(chips, CAP, width)
    swapped = lax.ppermute(outgoing[half:], "expert", core_pairs).reshape(chips, CAP, width)
    blocks = jnp.concatenate([kept, swapped], axis=1)
    chunk_a = blocks[0]
    chunk_b = [lax.ppermute(blocks[shift], "expert", chip_pairs(shift)) for shift in range(1, chips)]
    chunk_b = jnp.concatenate(chunk_b, axis=0)
    parts_a = gather_ring(chunk_a, shards)
    parts_b = gather_ring(chunk_b, shards)
    rows = jnp.concatenate(parts_b + parts_a, axis=0)

    gate_proj = jnp.dot(rows, w_gate[0], preferred_element_type=jnp.float32)
    up_proj = jnp.dot(rows, w_up[0], preferred_element_type=jnp.float32)
    hidden = (jax.nn.silu(gate_proj) * up_proj).astype(jnp.bfloat16)
    partial = jnp.dot(hidden, w_down[0], preferred_element_type=jnp.float32).astype(jnp.bfloat16)

    size_b, size_a = chunk_b.shape[0], chunk_a.shape[0]
    back_b = [partial[i * size_b:(i + 1) * size_b] for i in range(shards)]
    rest = partial[shards * size_b:]
    back_a = [rest[i * size_a:(i + 1) * size_a] for i in range(shards)]
    sum_b = scatter_ring(back_b, shards)
    sum_a = scatter_ring(back_a, shards)
    home = [sum_a]
    for shift in range(1, chips):
        home.append(
            lax.ppermute(
                sum_b[(shift - 1) * 2 * CAP:shift * 2 * CAP], "expert", chip_pairs(chips - shift)
            )
        )
    home = jnp.stack(home)
    mine = home[:, :CAP].reshape(half, width)
    other = lax.ppermute(home[:, CAP:].reshape(half, width), "expert", core_pairs)
    expert_out = jnp.concatenate([mine, other], axis=0)

    combine = (select.astype(jnp.float32) * route_weight.T[:, None, :]).reshape(window * CAP, -1)
    high = lax.reduce_precision(combine, 8, 7)
    low = combine - high
    mixed = jnp.einsum(
        "ct,cd->td",
        jnp.concatenate([high, low], axis=0).astype(jnp.bfloat16),
        jnp.concatenate([expert_out, expert_out], axis=0),
        preferred_element_type=jnp.float32,
    )
    return mixed.astype(jnp.bfloat16)


def solution(mesh):
    placed = (
        P(("groups", "expert", "dp"), None),
        P(("groups", "expert", "dp"), None),
        P(("groups", "expert", "dp"), None),
        P("expert", None, "dp"),
        P("expert", None, "dp"),
        P("expert", "dp", None),
    )
    return jax.shard_map(
        local,
        mesh=mesh,
        in_specs=placed,
        out_specs=P(("groups", "expert", "dp"), None),
        check_vma=False,
    )
```

```python
import functools

import jax
import jax.numpy as jnp
from jax import lax
from jax.experimental import pallas as pl
from jax.experimental.pallas import tpu as pltpu
from jax.sharding import PartitionSpec as P

CAP = 4
CORES = 2


def routing(expert_ids, gate_weights, experts):
    matches = expert_ids[:, :, None] == experts[None, None, :]
    chosen = jnp.any(matches, axis=1)
    weight = jnp.sum(jnp.where(matches, gate_weights[:, :, None], jnp.float32(0.0)), axis=1)
    count = chosen.astype(jnp.int32)
    tokens = count.shape[0]
    before = lax.broadcasted_iota(jnp.int32, (tokens, tokens), 0) > lax.broadcasted_iota(jnp.int32, (tokens, tokens), 1)
    position = jnp.dot(
        before.astype(jnp.bfloat16), count.astype(jnp.bfloat16), preferred_element_type=jnp.float32
    ).astype(jnp.int32)
    slot = jnp.arange(CAP, dtype=jnp.int32)
    select = (position.T[:, None, :] == slot[None, :, None]) & chosen.T[:, None, :]
    return select, weight


def ffn_kernel(rows_ref, gate_ref, up_ref, down_ref, out_ref):
    rows = rows_ref[...]
    gate = jnp.dot(rows, gate_ref[0], preferred_element_type=jnp.float32)
    up = jnp.dot(rows, up_ref[0], preferred_element_type=jnp.float32)
    hidden = (gate / (1.0 + jnp.exp(-gate)) * up).astype(jnp.bfloat16)
    width = out_ref.shape[1]
    tile = 1024
    for start in range(0, width, tile):
        out_ref[:, start:start + tile] = jnp.dot(
            hidden, down_ref[0, :, start:start + tile], preferred_element_type=jnp.float32
        ).astype(out_ref.dtype)


def hold_kernel(from_ref, to_ref, sem):
    copy = pltpu.make_async_copy(from_ref, to_ref, sem)
    copy.start()
    copy.wait()


def hold(weight):
    return pl.pallas_call(
        hold_kernel,
        out_shape=pltpu.VMEM(weight.shape, weight.dtype),
        in_specs=[pl.BlockSpec(memory_space=pltpu.HBM)],
        out_specs=pl.BlockSpec(memory_space=pltpu.VMEM),
        scratch_shapes=[pltpu.SemaphoreType.DMA],
        compiler_params=pltpu.CompilerParams(vmem_limit_bytes=1024 * 1024),
        cost_estimate=pl.CostEstimate(flops=0, bytes_accessed=4 * weight.size, transcendentals=0),
    )(weight)


def ffn(rows, w_gate, w_up, w_down):
    vmem = pl.BlockSpec(memory_space=pltpu.VMEM)
    held = [pltpu.with_memory_space_constraint(w, pltpu.VMEM) for w in (w_gate, w_up, w_down)]
    units = w_gate.shape[2]
    return pl.pallas_call(
        ffn_kernel,
        out_shape=jax.ShapeDtypeStruct(rows.shape, jnp.bfloat16),
        in_specs=[vmem] * 4,
        out_specs=vmem,
        compiler_params=pltpu.CompilerParams(vmem_limit_bytes=8 * 1024 * 1024),
        cost_estimate=pl.CostEstimate(
            flops=6 * rows.shape[0] * rows.shape[1] * units,
            bytes_accessed=2 * (3 * rows.shape[1] * units),
            transcendentals=rows.shape[0] * units,
        ),
    )(rows, *held)


def local(tokens, expert_ids, gate_weights, w_gate, w_up, w_down):
    window = lax.axis_size("expert")
    shards = lax.axis_size("dp")
    chips = window // CORES
    width = tokens.shape[1]
    me = lax.axis_index("expert")
    chip, core = me // CORES, me % CORES
    offset = jnp.arange(window, dtype=jnp.int32)
    core_offset, chip_offset = offset // chips, offset % chips
    experts = ((chip + chip_offset) % chips) * CORES + (core + core_offset) % CORES
    select, route_weight = routing(expert_ids, gate_weights, experts)
    flat_select = select.reshape(window * CAP, -1)
    outgoing = jnp.dot(
        flat_select.astype(jnp.bfloat16), tokens, preferred_element_type=jnp.float32
    ).astype(jnp.bfloat16)

    core_pairs = [(i, i ^ 1) for i in range(window)]

    def chip_pairs(shift):
        return [
            (c * CORES + k, ((c + shift) % chips) * CORES + k) for c in range(chips) for k in range(CORES)
        ]

    def along_dp(block, shift):
        return lax.ppermute(block, "dp", [(i, (i + shift) % shards) for i in range(shards)])

    shifts = sorted(range(1, shards), key=lambda s: abs(s - shards / 2))

    half = chips * CAP
    kept = outgoing[:half].reshape(chips, CAP, width)
    swapped = lax.ppermute(outgoing[half:], "expert", core_pairs).reshape(chips, CAP, width)
    blocks = jnp.concatenate([kept, swapped], axis=1)
    chunk_a = blocks[0]
    chunk_b = [lax.ppermute(blocks[shift], "expert", chip_pairs(shift)) for shift in range(1, chips)]
    parts_a = {0: chunk_a}
    for shift in shifts:
        parts_a[shift] = along_dp(chunk_a, shift)
    chunk_b = jnp.concatenate(chunk_b, axis=0)
    parts_b = {0: chunk_b}
    for shift in shifts:
        parts_b[shift] = along_dp(chunk_b, shift)
    order = [0] + shifts
    rows = jnp.concatenate([parts_a[s] for s in order] + [parts_b[s] for s in order], axis=0)

    w_gate, w_up, w_down, _ = lax.optimization_barrier((w_gate, w_up, w_down, chunk_b))
    partial = ffn(rows, hold(w_gate), hold(w_up), hold(w_down))

    size_b, size_a = chunk_b.shape[0], chunk_a.shape[0]

    def sum_over_dp(parts, size):
        arrived = [along_dp(parts[i * size:(i + 1) * size], shards - s) for i, s in enumerate(order) if s]
        total = parts[:size].astype(jnp.float32)
        for block in arrived:
            total = total + block.astype(jnp.float32)
        return total.astype(jnp.bfloat16)

    sum_b = sum_over_dp(partial[shards * size_a:], size_b)
    sum_a = sum_over_dp(partial[:shards * size_a], size_a)
    home = [sum_a]
    for shift in range(1, chips):
        home.append(
            lax.ppermute(
                sum_b[(shift - 1) * 2 * CAP:shift * 2 * CAP], "expert", chip_pairs(chips - shift)
            )
        )
    home = jnp.stack(home)
    mine = home[:, :CAP].reshape(half, width)
    other = lax.ppermute(home[:, CAP:].reshape(half, width), "expert", core_pairs)
    expert_out = jnp.concatenate([mine, other], axis=0)

    combine = (select.astype(jnp.float32) * route_weight.T[:, None, :]).reshape(window * CAP, -1)
    high = lax.reduce_precision(combine, 8, 7)
    low = combine - high
    mixed = jnp.einsum(
        "ct,cd->td",
        jnp.concatenate([high, low], axis=0).astype(jnp.bfloat16),
        jnp.concatenate([expert_out, expert_out], axis=0),
        preferred_element_type=jnp.float32,
    )
    return mixed.astype(jnp.bfloat16)


def solution(mesh):
    placed = (
        P(("groups", "expert", "dp"), None),
        P(("groups", "expert", "dp"), None),
        P(("groups", "expert", "dp"), None),
        P("expert", None, "dp"),
        P("expert", None, "dp"),
        P("expert", "dp", None),
    )
    return jax.shard_map(
        local,
        mesh=mesh,
        in_specs=placed,
        out_specs=P(("groups", "expert", "dp"), None),
        check_vma=False,
    )
```

```python
import functools

import jax
import jax.numpy as jnp
from jax import lax
from jax.experimental import pallas as pl
from jax.experimental.pallas import tpu as pltpu
from jax.sharding import PartitionSpec as P

CAP = 4
CORES = 2


def routing(expert_ids, gate_weights, experts):
    matches = expert_ids[:, :, None] == experts[None, None, :]
    chosen = jnp.any(matches, axis=1)
    weight = jnp.sum(jnp.where(matches, gate_weights[:, :, None], jnp.float32(0.0)), axis=1)
    count = chosen.astype(jnp.int32)
    tokens = count.shape[0]
    before = lax.broadcasted_iota(jnp.int32, (tokens, tokens), 0) > lax.broadcasted_iota(jnp.int32, (tokens, tokens), 1)
    position = jnp.dot(
        before.astype(jnp.bfloat16), count.astype(jnp.bfloat16), preferred_element_type=jnp.float32
    ).astype(jnp.int32)
    slot = jnp.arange(CAP, dtype=jnp.int32)
    select = (position.T[:, None, :] == slot[None, :, None]) & chosen.T[:, None, :]
    return select, weight


PIECES = 4
STEPS = 4


def hold_kernel(gate_from, up_from, gate_to, up_to, sems):
    copies = []
    for which, (source, target) in enumerate(((gate_from, gate_to), (up_from, up_to))):
        rows = source.shape[1] // PIECES
        for piece in range(PIECES):
            at = pl.ds(piece * rows, rows)
            copies.append(
                pltpu.make_async_copy(source.at[:, at], target.at[:, at], sems.at[which, piece])
            )
    for copy in copies:
        copy.start()
    for copy in copies:
        copy.wait()


def hold(w_gate, w_up):
    in_hbm = [pltpu.with_memory_space_constraint(w, pltpu.HBM) for w in (w_gate, w_up)]
    return pl.pallas_call(
        hold_kernel,
        out_shape=[pltpu.VMEM(w.shape, w.dtype) for w in (w_gate, w_up)],
        in_specs=[pl.BlockSpec(memory_space=pltpu.HBM)] * 2,
        out_specs=[pl.BlockSpec(memory_space=pltpu.VMEM)] * 2,
        scratch_shapes=[pltpu.SemaphoreType.DMA((2, PIECES))],
        compiler_params=pltpu.CompilerParams(vmem_limit_bytes=1024 * 1024),
        cost_estimate=pl.CostEstimate(flops=0, bytes_accessed=4 * w_gate.size, transcendentals=0),
    )(*in_hbm)


def ffn_kernel(rows_ref, gate_ref, up_ref, down_hbm, out_ref, down_ref, gate_sum, up_sum, sems):
    units = down_hbm.shape[1] // PIECES
    copies = []
    for piece in range(PIECES):
        at = pl.ds(piece * units, units)
        copies.append(pltpu.make_async_copy(down_hbm.at[0, at], down_ref.at[at], sems.at[piece]))
    for copy in copies:
        copy.start()
    depth = rows_ref.shape[1] // STEPS
    gate_sum[...] = jnp.zeros_like(gate_sum)
    up_sum[...] = jnp.zeros_like(up_sum)

    @pl.loop(0, STEPS)
    def _(step):
        at = pl.ds(pl.multiple_of(step * depth, 128), depth)
        rows = rows_ref[:, at]
        gate_sum[...] += jnp.dot(rows, gate_ref[0, at], preferred_element_type=jnp.float32)
        up_sum[...] += jnp.dot(rows, up_ref[0, at], preferred_element_type=jnp.float32)

    gate, up = gate_sum[...], up_sum[...]
    hidden = (gate / (1.0 + jnp.exp(-gate)) * up).astype(jnp.bfloat16)
    for copy in copies:
        copy.wait()
    width = out_ref.shape[1]
    tile = 1024
    for start in range(0, width, tile):
        out_ref[:, start:start + tile] = jnp.dot(
            hidden, down_ref[:, start:start + tile], preferred_element_type=jnp.float32
        ).astype(out_ref.dtype)


def ffn(rows, gate, up, w_down):
    vmem = pl.BlockSpec(memory_space=pltpu.VMEM)
    units, width = w_down.shape[1:]
    return pl.pallas_call(
        ffn_kernel,
        out_shape=jax.ShapeDtypeStruct(rows.shape, jnp.bfloat16),
        in_specs=[vmem] * 3 + [pl.BlockSpec(memory_space=pltpu.HBM)],
        out_specs=vmem,
        scratch_shapes=[
            pltpu.VMEM((units, width), w_down.dtype),
            pltpu.VMEM((rows.shape[0], units), jnp.float32),
            pltpu.VMEM((rows.shape[0], units), jnp.float32),
            pltpu.SemaphoreType.DMA((PIECES,)),
        ],
        compiler_params=pltpu.CompilerParams(vmem_limit_bytes=16 * 1024 * 1024),
        cost_estimate=pl.CostEstimate(
            flops=6 * rows.shape[0] * width * units,
            bytes_accessed=2 * width * units,
            transcendentals=rows.shape[0] * units,
        ),
    )(
        rows,
        pltpu.with_memory_space_constraint(gate, pltpu.VMEM),
        pltpu.with_memory_space_constraint(up, pltpu.VMEM),
        pltpu.with_memory_space_constraint(w_down, pltpu.HBM),
    )


def local(tokens, expert_ids, gate_weights, w_gate, w_up, w_down):
    window = lax.axis_size("expert")
    shards = lax.axis_size("dp")
    chips = window // CORES
    width = tokens.shape[1]
    me = lax.axis_index("expert")
    chip, core = me // CORES, me % CORES
    offset = jnp.arange(window, dtype=jnp.int32)
    core_offset, chip_offset = offset // chips, offset % chips
    experts = ((chip + chip_offset) % chips) * CORES + (core + core_offset) % CORES
    select, route_weight = routing(expert_ids, gate_weights, experts)
    flat_select = select.reshape(window * CAP, -1)
    outgoing = jnp.dot(
        flat_select.astype(jnp.bfloat16), tokens, preferred_element_type=jnp.float32
    ).astype(jnp.bfloat16)

    core_pairs = [(i, i ^ 1) for i in range(window)]

    def travel(block, chip_shift, dp_shift):
        pairs = []
        for c in range(chips):
            for k in range(CORES):
                for z in range(shards):
                    to_chip, to_shard = (c + chip_shift) % chips, (z + dp_shift) % shards
                    pairs.append(((c * CORES + k) * shards + z, (to_chip * CORES + k) * shards + to_shard))
        return lax.ppermute(block, ("expert", "dp"), pairs)

    ways = [(x, z) for z in sorted(range(shards), key=lambda z: -min(z, shards - z)) for x in range(chips)]

    half = chips * CAP
    kept = outgoing[:half].reshape(chips, CAP, width)
    swapped = lax.ppermute(outgoing[half:], "expert", core_pairs).reshape(chips, CAP, width)
    blocks = jnp.concatenate([kept, swapped], axis=1)
    arrived = [travel(blocks[x], x, z) if (x, z) != (0, 0) else blocks[0] for x, z in ways]
    rows = jnp.concatenate(arrived, axis=0)

    w_gate, w_up, _ = lax.optimization_barrier((w_gate, w_up, swapped))
    partial = ffn(rows, *hold(w_gate, w_up), w_down)

    partial = partial.reshape(len(ways), CORES * CAP, width)
    returned = {
        way: travel(partial[i], (chips - way[0]) % chips, (shards - way[1]) % shards) if way != (0, 0) else partial[i]
        for i, way in enumerate(ways)
    }
    home = []
    for x in range(chips):
        total = returned[x, 0].astype(jnp.float32)
        for z in range(1, shards):
            total = total + returned[x, z].astype(jnp.float32)
        home.append(total.astype(jnp.bfloat16))
    home = jnp.stack(home)
    mine = home[:, :CAP].reshape(half, width)
    other = lax.ppermute(home[:, CAP:].reshape(half, width), "expert", core_pairs)
    expert_out = jnp.concatenate([mine, other], axis=0)

    combine = (select.astype(jnp.float32) * route_weight.T[:, None, :]).reshape(window * CAP, -1)
    high = lax.reduce_precision(combine, 8, 7)
    low = combine - high
    mixed = jnp.einsum(
        "ct,cd->td",
        jnp.concatenate([high, low], axis=0).astype(jnp.bfloat16),
        jnp.concatenate([expert_out, expert_out], axis=0),
        preferred_element_type=jnp.float32,
    )
    return mixed.astype(jnp.bfloat16)


def solution(mesh):
    placed = (
        P(("groups", "expert", "dp"), None),
        P(("groups", "expert", "dp"), None),
        P(("groups", "expert", "dp"), None),
        P("expert", None, "dp"),
        P("expert", None, "dp"),
        P("expert", "dp", None),
    )
    return jax.shard_map(
        local,
        mesh=mesh,
        in_specs=placed,
        out_specs=P(("groups", "expert", "dp"), None),
        check_vma=False,
    )
```

```python
import functools

import jax
import jax.numpy as jnp
from jax import lax
from jax.experimental import pallas as pl
from jax.experimental.pallas import tpu as pltpu
from jax.sharding import PartitionSpec as P

CAP = 4
CORES = 2


def routing(expert_ids, gate_weights, experts):
    matches = expert_ids[:, :, None] == experts[None, None, :]
    chosen = jnp.any(matches, axis=1)
    weight = jnp.sum(jnp.where(matches, gate_weights[:, :, None], jnp.float32(0.0)), axis=1)
    count = chosen.astype(jnp.int32)
    tokens = count.shape[0]
    before = lax.broadcasted_iota(jnp.int32, (tokens, tokens), 0) > lax.broadcasted_iota(jnp.int32, (tokens, tokens), 1)
    position = jnp.dot(
        before.astype(jnp.bfloat16), count.astype(jnp.bfloat16), preferred_element_type=jnp.float32
    ).astype(jnp.int32)
    slot = jnp.arange(CAP, dtype=jnp.int32)
    select = (position.T[:, None, :] == slot[None, :, None]) & chosen.T[:, None, :]
    return select, weight


PIECES = 4
STEPS = 4


def hold_kernel(gate_from, up_from, gate_to, up_to, sems):
    copies = []
    for which, (source, target) in enumerate(((gate_from, gate_to), (up_from, up_to))):
        rows = source.shape[1] // PIECES
        for piece in range(PIECES):
            at = pl.ds(piece * rows, rows)
            copies.append(
                pltpu.make_async_copy(source.at[:, at], target.at[:, at], sems.at[which, piece])
            )
    for copy in copies:
        copy.start()
    for copy in copies:
        copy.wait()


def hold(w_gate, w_up):
    in_hbm = [pltpu.with_memory_space_constraint(w, pltpu.HBM) for w in (w_gate, w_up)]
    return pl.pallas_call(
        hold_kernel,
        out_shape=[pltpu.VMEM(w.shape, w.dtype) for w in (w_gate, w_up)],
        in_specs=[pl.BlockSpec(memory_space=pltpu.HBM)] * 2,
        out_specs=[pl.BlockSpec(memory_space=pltpu.VMEM)] * 2,
        scratch_shapes=[pltpu.SemaphoreType.DMA((2, PIECES))],
        compiler_params=pltpu.CompilerParams(vmem_limit_bytes=1024 * 1024),
        cost_estimate=pl.CostEstimate(flops=0, bytes_accessed=4 * w_gate.size, transcendentals=0),
    )(*in_hbm)


def ffn_kernel(rows_ref, gate_ref, up_ref, down_hbm, *refs):
    out_refs, (down_ref, gate_sum, up_sum, sems) = refs[:-4], refs[-4:]
    units = down_hbm.shape[1] // PIECES
    copies = []
    for piece in range(PIECES):
        at = pl.ds(piece * units, units)
        copies.append(pltpu.make_async_copy(down_hbm.at[0, at], down_ref.at[at], sems.at[piece]))
    for copy in copies:
        copy.start()
    depth = rows_ref.shape[1] // STEPS
    gate_sum[...] = jnp.zeros_like(gate_sum)
    up_sum[...] = jnp.zeros_like(up_sum)

    @pl.loop(0, STEPS)
    def _(step):
        at = pl.ds(pl.multiple_of(step * depth, 128), depth)
        rows = rows_ref[:, at]
        gate_sum[...] += jnp.dot(rows, gate_ref[0, at], preferred_element_type=jnp.float32)
        up_sum[...] += jnp.dot(rows, up_ref[0, at], preferred_element_type=jnp.float32)

    gate, up = gate_sum[...], up_sum[...]
    hidden = (gate / (1.0 + jnp.exp(-gate)) * up).astype(jnp.bfloat16)
    for copy in copies:
        copy.wait()
    part, width = out_refs[0].shape
    tile = 1024
    for start in range(0, width, tile):
        product = jnp.dot(hidden, down_ref[:, start:start + tile], preferred_element_type=jnp.float32)
        for i, out_ref in enumerate(out_refs):
            out_ref[:, start:start + tile] = product[i * part:(i + 1) * part].astype(out_ref.dtype)


def ffn(rows, gate, up, w_down, part):
    vmem = pl.BlockSpec(memory_space=pltpu.VMEM)
    units, width = w_down.shape[1:]
    return pl.pallas_call(
        ffn_kernel,
        out_shape=[jax.ShapeDtypeStruct((part, width), jnp.bfloat16)] * (rows.shape[0] // part),
        in_specs=[vmem] * 3 + [pl.BlockSpec(memory_space=pltpu.HBM)],
        out_specs=[vmem] * (rows.shape[0] // part),
        scratch_shapes=[
            pltpu.VMEM((units, width), w_down.dtype),
            pltpu.VMEM((rows.shape[0], units), jnp.float32),
            pltpu.VMEM((rows.shape[0], units), jnp.float32),
            pltpu.SemaphoreType.DMA((PIECES,)),
        ],
        compiler_params=pltpu.CompilerParams(vmem_limit_bytes=16 * 1024 * 1024),
        cost_estimate=pl.CostEstimate(
            flops=6 * rows.shape[0] * width * units,
            bytes_accessed=2 * width * units,
            transcendentals=rows.shape[0] * units,
        ),
    )(
        rows,
        pltpu.with_memory_space_constraint(gate, pltpu.VMEM),
        pltpu.with_memory_space_constraint(up, pltpu.VMEM),
        pltpu.with_memory_space_constraint(w_down, pltpu.HBM),
    )


def local(tokens, expert_ids, gate_weights, w_gate, w_up, w_down):
    window = lax.axis_size("expert")
    shards = lax.axis_size("dp")
    chips = window // CORES
    width = tokens.shape[1]
    me = lax.axis_index("expert")
    chip, core = me // CORES, me % CORES
    offset = jnp.arange(window, dtype=jnp.int32)
    core_offset, chip_offset = offset // chips, offset % chips
    experts = ((chip + chip_offset) % chips) * CORES + (core + core_offset) % CORES
    select, route_weight = routing(expert_ids, gate_weights, experts)
    flat_select = select.reshape(window * CAP, -1)
    outgoing = jnp.dot(
        flat_select.astype(jnp.bfloat16), tokens, preferred_element_type=jnp.float32
    ).astype(jnp.bfloat16)

    core_pairs = [(i, i ^ 1) for i in range(window)]

    def travel(block, chip_shift, dp_bit):
        pairs = []
        for c in range(chips):
            for k in range(CORES):
                for z in range(shards):
                    to_chip = (c + chip_shift) % chips
                    pairs.append(((c * CORES + k) * shards + z, (to_chip * CORES + k) * shards + (z ^ dp_bit)))
        return lax.ppermute(block, ("expert", "dp"), pairs)

    bits = [1 << i for i in range((shards - 1).bit_length())]

    half = chips * CAP
    kept = outgoing[:half].reshape(chips, CAP, width)
    swapped = lax.ppermute(outgoing[half:], "expert", core_pairs).reshape(chips, CAP, width)
    blocks = jnp.concatenate([kept, swapped], axis=1)
    size = CORES * CAP
    others = [travel(blocks[x], x, 0) for x in range(1, chips)]
    own = jnp.concatenate([blocks[0]] + others, axis=0)
    held = [{0: own[x * size:(x + 1) * size] if x else blocks[0]} for x in range(chips)]
    for bit in reversed(bits[1:]):
        for blocks_of in held:
            blocks_of.update({offset ^ bit: travel(blocks_of[offset], 0, bit) for offset in list(blocks_of)})
    near = travel(own, 0, 1) if shards > 1 else None
    passed = [
        (x, offset ^ 1, travel(held[x][offset], 0, 1)) for x in range(chips) for offset in held[x] if offset and shards > 1
    ]
    ways = [(x, 0) for x in range(chips)] + [(x, 1) for x in range(chips) if shards > 1]
    ways += [(x, offset) for x in range(chips) for offset in held[x] if offset]
    ways += [(x, offset) for x, offset, _ in passed]
    pieces = [own] + ([near] if shards > 1 else [])
    pieces += [held[x][offset] for x in range(chips) for offset in held[x] if offset]
    rows = jnp.concatenate(pieces + [block for _, _, block in passed], axis=0)

    w_gate, w_up, _ = lax.optimization_barrier((w_gate, w_up, own))
    partial = ffn(rows, *hold(w_gate, w_up), w_down, size)

    parts = dict(zip(ways, partial))
    home = {x: [] for x in range(chips)}
    relayed = []
    last = [(x, 0, 0) for x in range(chips)]
    for bit in bits:
        for x in reversed(range(chips)):
            for offset in [o for o in reversed(range(shards)) if (x, o) in parts and o & bit]:
                if offset == bit:
                    last.append((x, offset, bit))
                else:
                    arrived = travel(parts.pop((x, offset)), 0, bit)
                    onward = (x, offset ^ bit)
                    parts[onward] = (parts[onward].astype(jnp.float32) + arrived.astype(jnp.float32)).astype(jnp.bfloat16)
                    relayed.append(arrived)
    plain = [(x, offset) for x, offset, bit in last if offset <= 1 and relayed and (x or offset)]
    waited, _ = lax.optimization_barrier(([parts[way] for way in plain], relayed))
    parts.update(zip(plain, waited))
    for x, offset, bit in last:
        shift = (chips - x) % chips
        block = parts[x, offset]
        home[x].append(travel(block, shift, bit) if shift or bit else block)
    home = jnp.stack([sum(block.astype(jnp.float32) for block in home[x]).astype(jnp.bfloat16) for x in range(chips)])
    mine = home[:, :CAP].reshape(half, width)
    other = lax.ppermute(home[:, CAP:].reshape(half, width), "expert", core_pairs)
    expert_out = jnp.concatenate([mine, other], axis=0)

    combine = (select.astype(jnp.float32) * route_weight.T[:, None, :]).reshape(window * CAP, -1)
    high = lax.reduce_precision(combine, 8, 7)
    low = combine - high
    mixed = jnp.einsum(
        "ct,cd->td",
        jnp.concatenate([high, low], axis=0).astype(jnp.bfloat16),
        jnp.concatenate([expert_out, expert_out], axis=0),
        preferred_element_type=jnp.float32,
    )
    return mixed.astype(jnp.bfloat16)


def solution(mesh):
    placed = (
        P(("groups", "expert", "dp"), None),
        P(("groups", "expert", "dp"), None),
        P(("groups", "expert", "dp"), None),
        P("expert", None, "dp"),
        P("expert", None, "dp"),
        P("expert", "dp", None),
    )
    return jax.shard_map(
        local,
        mesh=mesh,
        in_specs=placed,
        out_specs=P(("groups", "expert", "dp"), None),
        check_vma=False,
    )
```

```python
import functools

import jax
import jax.numpy as jnp
from jax import lax
from jax.experimental import pallas as pl
from jax.experimental.pallas import tpu as pltpu
from jax.sharding import PartitionSpec as P

CAP = 4
CORES = 2


def route_kernel(chips, *refs):
    sources, (kept_ref, sent_ref, mix_ref), (ids_ref, weights_ref, tokens_ref, sems) = refs[:3], refs[3:6], refs[6:]
    copies = [
        pltpu.make_async_copy(source, target, sems.at[i])
        for i, (source, target) in enumerate(zip(sources, (ids_ref, weights_ref, tokens_ref)))
    ]
    for copy in copies:
        copy.start()
    me = lax.axis_index("expert")
    chip, core = me // CORES, me % CORES
    slots = CORES * chips * CAP
    topk, tokens = ids_ref.shape
    row = lax.broadcasted_iota(jnp.int32, (slots, tokens), 0)
    expert = jnp.zeros_like(row)
    for i in range(CORES * chips):
        core_offset, chip_offset = i // chips, i % chips
        named = lax.rem(chip + chip_offset, chips) * CORES + lax.rem(core + core_offset, CORES)
        expert = jnp.where((row >= i * CAP) & (row < (i + 1) * CAP), named, expert)
    copies[0].wait()
    copies[1].wait()
    chosen = jnp.zeros((slots, tokens), jnp.float32)
    weight = jnp.zeros((slots, tokens), jnp.float32)
    for k in range(topk):
        hit = ids_ref[k:k + 1, :] == expert
        chosen = jnp.where(hit, 1.0, chosen)
        weight = weight + jnp.where(hit, weights_ref[k:k + 1, :], 0.0)
    before = lax.broadcasted_iota(jnp.int32, (tokens, tokens), 0) < lax.broadcasted_iota(jnp.int32, (tokens, tokens), 1)
    position = jnp.dot(
        chosen.astype(jnp.bfloat16), jnp.where(before, 1.0, 0.0).astype(jnp.bfloat16), preferred_element_type=jnp.float32
    )
    slot = (row & (CAP - 1)).astype(jnp.float32)
    select = jnp.where(position == slot, chosen, 0.0)
    combine = select * weight
    high = combine.astype(jnp.bfloat16)
    mix_ref[:slots] = high
    mix_ref[slots:] = (combine - high.astype(jnp.float32)).astype(jnp.bfloat16)
    select = select.astype(jnp.bfloat16)
    copies[2].wait()
    half, width = kept_ref.shape
    tile = 1024
    for start in range(0, width, tile):
        picked = jnp.dot(select, tokens_ref[:, start:start + tile], preferred_element_type=jnp.float32)
        kept_ref[:, start:start + tile] = picked[:half].astype(jnp.bfloat16)
        sent_ref[:, start:start + tile] = picked[half:].astype(jnp.bfloat16)


def route(tokens, expert_ids, gate_weights, chips):
    vmem = pl.BlockSpec(memory_space=pltpu.VMEM)
    count, width = tokens.shape
    half = chips * CAP
    arrays = (expert_ids.T, gate_weights.T, tokens)
    return pl.pallas_call(
        functools.partial(route_kernel, chips),
        out_shape=[
            jax.ShapeDtypeStruct((half, width), jnp.bfloat16),
            jax.ShapeDtypeStruct((half, width), jnp.bfloat16),
            jax.ShapeDtypeStruct((2 * CORES * half, count), jnp.bfloat16),
        ],
        in_specs=[pl.BlockSpec(memory_space=pltpu.HBM)] * 3,
        out_specs=[vmem] * 3,
        scratch_shapes=[pltpu.VMEM(array.shape, array.dtype) for array in arrays] + [pltpu.SemaphoreType.DMA((3,))],
        compiler_params=pltpu.CompilerParams(vmem_limit_bytes=8 * 1024 * 1024),
        cost_estimate=pl.CostEstimate(
            flops=4 * half * CORES * count * width, bytes_accessed=4 * count * width, transcendentals=0
        ),
    )(*[pltpu.with_memory_space_constraint(array, pltpu.HBM) for array in arrays])


PIECES = 4
STEPS = 4


def hold_kernel(source, target, sems):
    rows = source.shape[1] // PIECES
    copies = []
    for piece in range(PIECES):
        at = pl.ds(piece * rows, rows)
        copies.append(pltpu.make_async_copy(source.at[:, at], target.at[:, at], sems.at[piece]))
    for copy in copies:
        copy.start()
    for copy in copies:
        copy.wait()


def hold(weight):
    return pl.pallas_call(
        hold_kernel,
        out_shape=pltpu.VMEM(weight.shape, weight.dtype),
        in_specs=[pl.BlockSpec(memory_space=pltpu.HBM)],
        out_specs=pl.BlockSpec(memory_space=pltpu.VMEM),
        scratch_shapes=[pltpu.SemaphoreType.DMA((PIECES,))],
        compiler_params=pltpu.CompilerParams(vmem_limit_bytes=1024 * 1024),
        cost_estimate=pl.CostEstimate(flops=0, bytes_accessed=4 * weight.size, transcendentals=0),
    )(pltpu.with_memory_space_constraint(weight, pltpu.HBM))


def ffn_kernel(rows_ref, gate_ref, up_ref, down_hbm, *refs):
    out_refs, (down_ref, gate_sum, up_sum, sems) = refs[:-4], refs[-4:]
    units = down_hbm.shape[1] // PIECES
    copies = []
    for piece in range(PIECES):
        at = pl.ds(piece * units, units)
        copies.append(pltpu.make_async_copy(down_hbm.at[0, at], down_ref.at[at], sems.at[piece]))
    for copy in copies:
        copy.start()
    depth = rows_ref.shape[1] // STEPS
    gate_sum[...] = jnp.zeros_like(gate_sum)
    up_sum[...] = jnp.zeros_like(up_sum)

    @pl.loop(0, STEPS)
    def _(step):
        at = pl.ds(pl.multiple_of(step * depth, 128), depth)
        rows = rows_ref[:, at]
        gate_sum[...] += jnp.dot(rows, gate_ref[0, at], preferred_element_type=jnp.float32)
        up_sum[...] += jnp.dot(rows, up_ref[0, at], preferred_element_type=jnp.float32)

    gate, up = gate_sum[...], up_sum[...]
    hidden = (gate / (1.0 + jnp.exp(-gate)) * up).astype(jnp.bfloat16)
    for copy in copies:
        copy.wait()
    part, width = out_refs[0].shape
    tile = 1024
    for start in range(0, width, tile):
        product = jnp.dot(hidden, down_ref[:, start:start + tile], preferred_element_type=jnp.float32)
        for i, out_ref in enumerate(out_refs):
            out_ref[:, start:start + tile] = product[i * part:(i + 1) * part].astype(out_ref.dtype)


def ffn(rows, gate, up, w_down, part):
    vmem = pl.BlockSpec(memory_space=pltpu.VMEM)
    units, width = w_down.shape[1:]
    return pl.pallas_call(
        ffn_kernel,
        out_shape=[jax.ShapeDtypeStruct((part, width), jnp.bfloat16)] * (rows.shape[0] // part),
        in_specs=[vmem] * 3 + [pl.BlockSpec(memory_space=pltpu.HBM)],
        out_specs=[vmem] * (rows.shape[0] // part),
        scratch_shapes=[
            pltpu.VMEM((units, width), w_down.dtype),
            pltpu.VMEM((rows.shape[0], units), jnp.float32),
            pltpu.VMEM((rows.shape[0], units), jnp.float32),
            pltpu.SemaphoreType.DMA((PIECES,)),
        ],
        compiler_params=pltpu.CompilerParams(vmem_limit_bytes=16 * 1024 * 1024),
        cost_estimate=pl.CostEstimate(
            flops=6 * rows.shape[0] * width * units,
            bytes_accessed=2 * width * units,
            transcendentals=rows.shape[0] * units,
        ),
    )(
        rows,
        pltpu.with_memory_space_constraint(gate, pltpu.VMEM),
        pltpu.with_memory_space_constraint(up, pltpu.VMEM),
        pltpu.with_memory_space_constraint(w_down, pltpu.HBM),
    )


def local(tokens, expert_ids, gate_weights, w_gate, w_up, w_down):
    window = lax.axis_size("expert")
    shards = lax.axis_size("dp")
    chips = window // CORES
    width = tokens.shape[1]
    kept, sent, mix = route(tokens, expert_ids, gate_weights, chips)

    core_pairs = [(i, i ^ 1) for i in range(window)]

    def travel(block, chip_shift, dp_bit):
        pairs = []
        for c in range(chips):
            for k in range(CORES):
                for z in range(shards):
                    to_chip = (c + chip_shift) % chips
                    pairs.append(((c * CORES + k) * shards + z, (to_chip * CORES + k) * shards + (z ^ dp_bit)))
        return lax.ppermute(block, ("expert", "dp"), pairs)

    bits = [1 << i for i in range((shards - 1).bit_length())]

    half = chips * CAP
    swapped = lax.ppermute(sent, "expert", core_pairs).reshape(chips, CAP, width)
    blocks = jnp.concatenate([kept.reshape(chips, CAP, width), swapped], axis=1)
    size = CORES * CAP
    others = [travel(blocks[x], x, 0) for x in range(1, chips)]
    own = jnp.concatenate([blocks[0]] + others, axis=0)
    held = [{0: own[x * size:(x + 1) * size] if x else blocks[0]} for x in range(chips)]
    for bit in reversed(bits[1:]):
        for blocks_of in held:
            blocks_of.update({offset ^ bit: travel(blocks_of[offset], 0, bit) for offset in list(blocks_of)})
    near = travel(own, 0, 1) if shards > 1 else None
    passed = [
        (x, offset ^ 1, travel(held[x][offset], 0, 1)) for x in range(chips) for offset in held[x] if offset and shards > 1
    ]
    ways = [(x, 0) for x in range(chips)] + [(x, 1) for x in range(chips) if shards > 1]
    ways += [(x, offset) for x in range(chips) for offset in held[x] if offset]
    ways += [(x, offset) for x, offset, _ in passed]
    pieces = [own] + ([near] if shards > 1 else [])
    pieces += [held[x][offset] for x in range(chips) for offset in held[x] if offset]
    rows = jnp.concatenate(pieces + [block for _, _, block in passed], axis=0)

    w_up, _ = lax.optimization_barrier((w_up, own))
    partial = ffn(rows, w_gate, hold(w_up), w_down, size)

    parts = dict(zip(ways, partial))
    home = {x: [] for x in range(chips)}
    relayed = []
    last = [(x, 0, 0) for x in range(chips)]
    for bit in bits:
        for x in reversed(range(chips)):
            for offset in [o for o in reversed(range(shards)) if (x, o) in parts and o & bit]:
                if offset == bit:
                    last.append((x, offset, bit))
                else:
                    arrived = travel(parts.pop((x, offset)), 0, bit)
                    onward = (x, offset ^ bit)
                    parts[onward] = (parts[onward].astype(jnp.float32) + arrived.astype(jnp.float32)).astype(jnp.bfloat16)
                    relayed.append(arrived)
    plain = [(x, offset) for x, offset, bit in last if offset <= 1 and relayed and (x or offset)]
    waited, _ = lax.optimization_barrier(([parts[way] for way in plain], relayed))
    parts.update(zip(plain, waited))
    for x, offset, bit in last:
        shift = (chips - x) % chips
        block = parts[x, offset]
        home[x].append(travel(block, shift, bit) if shift or bit else block)
    home = jnp.stack([sum(block.astype(jnp.float32) for block in home[x]).astype(jnp.bfloat16) for x in range(chips)])
    mine = home[:, :CAP].reshape(half, width)
    other = lax.ppermute(home[:, CAP:].reshape(half, width), "expert", core_pairs)
    expert_out = jnp.concatenate([mine, other], axis=0)

    mixed = jnp.einsum(
        "ct,cd->td", mix, jnp.concatenate([expert_out, expert_out], axis=0), preferred_element_type=jnp.float32
    )
    return mixed.astype(jnp.bfloat16)


def solution(mesh):
    placed = (
        P(("groups", "expert", "dp"), None),
        P(("groups", "expert", "dp"), None),
        P(("groups", "expert", "dp"), None),
        P("expert", None, "dp"),
        P("expert", None, "dp"),
        P("expert", "dp", None),
    )
    return jax.shard_map(
        local,
        mesh=mesh,
        in_specs=placed,
        out_specs=P(("groups", "expert", "dp"), None),
        check_vma=False,
    )
```

```python
import functools

import jax
import jax.numpy as jnp
from jax import lax
from jax.experimental import pallas as pl
from jax.experimental.pallas import tpu as pltpu
from jax.sharding import PartitionSpec as P

CAP = 4
CORES = 2


def route_kernel(chips, *refs):
    sources, (kept_ref, sent_ref, mix_ref), (ids_ref, weights_ref, tokens_ref, sems) = refs[:3], refs[3:6], refs[6:]
    copies = [
        pltpu.make_async_copy(source, target, sems.at[i])
        for i, (source, target) in enumerate(zip(sources, (ids_ref, weights_ref, tokens_ref)))
    ]
    for copy in copies:
        copy.start()
    me = lax.axis_index("expert")
    chip, core = me // CORES, me % CORES
    slots = CORES * chips * CAP
    topk, tokens = ids_ref.shape
    row = lax.broadcasted_iota(jnp.int32, (slots, tokens), 0)
    expert = jnp.zeros_like(row)
    for i in range(CORES * chips):
        core_offset, chip_offset = i // chips, i % chips
        named = lax.rem(chip + chip_offset, chips) * CORES + lax.rem(core + core_offset, CORES)
        expert = jnp.where((row >= i * CAP) & (row < (i + 1) * CAP), named, expert)
    copies[0].wait()
    copies[1].wait()
    chosen = jnp.zeros((slots, tokens), jnp.float32)
    weight = jnp.zeros((slots, tokens), jnp.float32)
    for k in range(topk):
        hit = ids_ref[k:k + 1, :] == expert
        chosen = jnp.where(hit, 1.0, chosen)
        weight = weight + jnp.where(hit, weights_ref[k:k + 1, :], 0.0)
    before = lax.broadcasted_iota(jnp.int32, (tokens, tokens), 0) < lax.broadcasted_iota(jnp.int32, (tokens, tokens), 1)
    position = jnp.dot(
        chosen.astype(jnp.bfloat16), jnp.where(before, 1.0, 0.0).astype(jnp.bfloat16), preferred_element_type=jnp.float32
    )
    slot = (row & (CAP - 1)).astype(jnp.float32)
    select = jnp.where(position == slot, chosen, 0.0)
    combine = select * weight
    high = combine.astype(jnp.bfloat16)
    mix_ref[:slots] = high
    mix_ref[slots:] = (combine - high.astype(jnp.float32)).astype(jnp.bfloat16)
    select = select.astype(jnp.bfloat16)
    copies[2].wait()
    half, width = kept_ref.shape
    tile = 1024
    for start in range(0, width, tile):
        picked = jnp.dot(select, tokens_ref[:, start:start + tile], preferred_element_type=jnp.float32)
        kept_ref[:, start:start + tile] = picked[:half].astype(jnp.bfloat16)
        sent_ref[:, start:start + tile] = picked[half:].astype(jnp.bfloat16)


def route(tokens, expert_ids, gate_weights, chips):
    vmem = pl.BlockSpec(memory_space=pltpu.VMEM)
    count, width = tokens.shape
    half = chips * CAP
    arrays = (expert_ids.T, gate_weights.T, tokens)
    return pl.pallas_call(
        functools.partial(route_kernel, chips),
        out_shape=[
            jax.ShapeDtypeStruct((half, width), jnp.bfloat16),
            jax.ShapeDtypeStruct((half, width), jnp.bfloat16),
            jax.ShapeDtypeStruct((2 * CORES * half, count), jnp.bfloat16),
        ],
        in_specs=[pl.BlockSpec(memory_space=pltpu.HBM)] * 3,
        out_specs=[vmem] * 3,
        scratch_shapes=[pltpu.VMEM(array.shape, array.dtype) for array in arrays] + [pltpu.SemaphoreType.DMA((3,))],
        compiler_params=pltpu.CompilerParams(vmem_limit_bytes=8 * 1024 * 1024),
        cost_estimate=pl.CostEstimate(
            flops=4 * half * CORES * count * width, bytes_accessed=4 * count * width, transcendentals=0
        ),
    )(*[pltpu.with_memory_space_constraint(array, pltpu.HBM) for array in arrays])


PIECES = 4
STEPS = 4


def hold_kernel(source, target, sems):
    rows = source.shape[1] // PIECES
    copies = []
    for piece in range(PIECES):
        at = pl.ds(piece * rows, rows)
        copies.append(pltpu.make_async_copy(source.at[:, at], target.at[:, at], sems.at[piece]))
    for copy in copies:
        copy.start()
    for copy in copies:
        copy.wait()


def hold(weight):
    return pl.pallas_call(
        hold_kernel,
        out_shape=pltpu.VMEM(weight.shape, weight.dtype),
        in_specs=[pl.BlockSpec(memory_space=pltpu.HBM)],
        out_specs=pl.BlockSpec(memory_space=pltpu.VMEM),
        scratch_shapes=[pltpu.SemaphoreType.DMA((PIECES,))],
        compiler_params=pltpu.CompilerParams(vmem_limit_bytes=1024 * 1024),
        cost_estimate=pl.CostEstimate(flops=0, bytes_accessed=4 * weight.size, transcendentals=0),
    )(pltpu.with_memory_space_constraint(weight, pltpu.HBM))


def ffn_kernel(rows_ref, gate_ref, up_ref, down_hbm, *refs):
    out_refs, (down_ref, gate_sum, up_sum, sems) = refs[:-4], refs[-4:]
    units = down_hbm.shape[1] // PIECES
    copies = []
    for piece in range(PIECES):
        at = pl.ds(piece * units, units)
        copies.append(pltpu.make_async_copy(down_hbm.at[0, at], down_ref.at[at], sems.at[piece]))
    for copy in copies:
        copy.start()
    depth = rows_ref.shape[1] // STEPS
    gate_sum[...] = jnp.zeros_like(gate_sum)
    up_sum[...] = jnp.zeros_like(up_sum)

    @pl.loop(0, STEPS)
    def _(step):
        at = pl.ds(pl.multiple_of(step * depth, 128), depth)
        rows = rows_ref[:, at]
        gate_sum[...] += jnp.dot(rows, gate_ref[0, at], preferred_element_type=jnp.float32)
        up_sum[...] += jnp.dot(rows, up_ref[0, at], preferred_element_type=jnp.float32)

    gate, up = gate_sum[...], up_sum[...]
    hidden = (gate / (1.0 + jnp.exp(-gate)) * up).astype(jnp.bfloat16)
    for copy in copies:
        copy.wait()
    part, width = out_refs[0].shape
    tile = 1024
    for start in range(0, width, tile):
        product = jnp.dot(hidden, down_ref[:, start:start + tile], preferred_element_type=jnp.float32)
        for i, out_ref in enumerate(out_refs):
            out_ref[:, start:start + tile] = product[i * part:(i + 1) * part].astype(out_ref.dtype)


def ffn(rows, gate, up, w_down, part):
    vmem = pl.BlockSpec(memory_space=pltpu.VMEM)
    units, width = w_down.shape[1:]
    return pl.pallas_call(
        ffn_kernel,
        out_shape=[jax.ShapeDtypeStruct((part, width), jnp.bfloat16)] * (rows.shape[0] // part),
        in_specs=[vmem] * 3 + [pl.BlockSpec(memory_space=pltpu.HBM)],
        out_specs=[vmem] * (rows.shape[0] // part),
        scratch_shapes=[
            pltpu.VMEM((units, width), w_down.dtype),
            pltpu.VMEM((rows.shape[0], units), jnp.float32),
            pltpu.VMEM((rows.shape[0], units), jnp.float32),
            pltpu.SemaphoreType.DMA((PIECES,)),
        ],
        compiler_params=pltpu.CompilerParams(vmem_limit_bytes=16 * 1024 * 1024),
        cost_estimate=pl.CostEstimate(
            flops=6 * rows.shape[0] * width * units,
            bytes_accessed=2 * width * units,
            transcendentals=rows.shape[0] * units,
        ),
    )(
        rows,
        pltpu.with_memory_space_constraint(gate, pltpu.VMEM),
        pltpu.with_memory_space_constraint(up, pltpu.VMEM),
        pltpu.with_memory_space_constraint(w_down, pltpu.HBM),
    )


def local(tokens, expert_ids, gate_weights, w_gate, w_up, w_down):
    window = lax.axis_size("expert")
    shards = lax.axis_size("dp")
    chips = window // CORES
    width = tokens.shape[1]
    kept, sent, mix = route(tokens, expert_ids, gate_weights, chips)

    core_pairs = [(i, i ^ 1) for i in range(window)]

    def travel(block, chip_shift, dp_bit):
        pairs = []
        for c in range(chips):
            for k in range(CORES):
                for z in range(shards):
                    to_chip = (c + chip_shift) % chips
                    pairs.append(((c * CORES + k) * shards + z, (to_chip * CORES + k) * shards + (z ^ dp_bit)))
        return lax.ppermute(block, ("expert", "dp"), pairs)

    bits = [1 << i for i in range((shards - 1).bit_length())]

    half = chips * CAP
    swapped = lax.ppermute(sent, "expert", core_pairs).reshape(chips, CAP, width)
    blocks = jnp.concatenate([kept.reshape(chips, CAP, width), swapped], axis=1)
    size = CORES * CAP
    held = {0: blocks.reshape(chips * size, width)}
    for bit in reversed(bits[1:]):
        for offset in list(held):
            held[offset ^ bit] = [travel(held[offset][x * size:(x + 1) * size], 0, bit) for x in range(chips)]
            held[offset ^ bit] = jnp.concatenate(held[offset ^ bit], axis=0)
    ways, pieces = [], []
    for offset in list(held):
        for x in range(chips):
            block = held[offset][x * size:(x + 1) * size]
            for bit in [0] + bits[:1]:
                ways.append((x, offset ^ bit))
                pieces.append(travel(block, x, bit) if x or bit else block)
    rows = jnp.concatenate(pieces, axis=0)

    w_up, _ = lax.optimization_barrier((w_up, swapped))
    partial = ffn(rows, w_gate, hold(w_up), w_down, size)

    parts = dict(zip(ways, partial))
    home = {x: [] for x in range(chips)}
    relayed = []
    last = [(x, 0, 0) for x in range(chips)]
    for bit in bits:
        for x in reversed(range(chips)):
            for offset in [o for o in reversed(range(shards)) if (x, o) in parts and o & bit]:
                if offset == bit:
                    last.append((x, offset, bit))
                else:
                    arrived = travel(parts.pop((x, offset)), 0, bit)
                    onward = (x, offset ^ bit)
                    parts[onward] = (parts[onward].astype(jnp.float32) + arrived.astype(jnp.float32)).astype(jnp.bfloat16)
                    relayed.append(arrived)
    plain = [(x, offset) for x, offset, bit in last if offset <= 1 and relayed and (x or offset)]
    waited, _ = lax.optimization_barrier(([parts[way] for way in plain], relayed))
    parts.update(zip(plain, waited))
    for x, offset, bit in last:
        shift = (chips - x) % chips
        block = parts[x, offset]
        home[x].append(travel(block, shift, bit) if shift or bit else block)
    home = jnp.stack([sum(block.astype(jnp.float32) for block in home[x]).astype(jnp.bfloat16) for x in range(chips)])
    mine = home[:, :CAP].reshape(half, width)
    other = lax.ppermute(home[:, CAP:].reshape(half, width), "expert", core_pairs)
    expert_out = jnp.concatenate([mine, other], axis=0)

    mixed = jnp.einsum(
        "ct,cd->td", mix, jnp.concatenate([expert_out, expert_out], axis=0), preferred_element_type=jnp.float32
    )
    return mixed.astype(jnp.bfloat16)


def solution(mesh):
    placed = (
        P(("groups", "expert", "dp"), None),
        P(("groups", "expert", "dp"), None),
        P(("groups", "expert", "dp"), None),
        P("expert", None, "dp"),
        P("expert", None, "dp"),
        P("expert", "dp", None),
    )
    return jax.shard_map(
        local,
        mesh=mesh,
        in_specs=placed,
        out_specs=P(("groups", "expert", "dp"), None),
        check_vma=False,
    )
```

```python
import functools

import jax
import jax.numpy as jnp
from jax import lax
from jax.experimental import pallas as pl
from jax.experimental.pallas import tpu as pltpu
from jax.sharding import PartitionSpec as P

CAP = 4
CORES = 2


def route_kernel(chips, *refs):
    sources, (kept_ref, sent_ref, mix_ref), (ids_ref, weights_ref, tokens_ref, sems) = refs[:3], refs[3:6], refs[6:]
    copies = [
        pltpu.make_async_copy(source, target, sems.at[i])
        for i, (source, target) in enumerate(zip(sources, (ids_ref, weights_ref, tokens_ref)))
    ]
    for copy in copies:
        copy.start()
    me = lax.axis_index("expert")
    chip, core = me // CORES, me % CORES
    slots = CORES * chips * CAP
    topk, tokens = ids_ref.shape
    row = lax.broadcasted_iota(jnp.int32, (slots, tokens), 0)
    expert = jnp.zeros_like(row)
    for i in range(CORES * chips):
        core_offset, chip_offset = i // chips, i % chips
        named = lax.rem(chip + chip_offset, chips) * CORES + lax.rem(core + core_offset, CORES)
        expert = jnp.where((row >= i * CAP) & (row < (i + 1) * CAP), named, expert)
    copies[0].wait()
    copies[1].wait()
    chosen = jnp.zeros((slots, tokens), jnp.float32)
    weight = jnp.zeros((slots, tokens), jnp.float32)
    for k in range(topk):
        hit = ids_ref[k:k + 1, :] == expert
        chosen = jnp.where(hit, 1.0, chosen)
        weight = weight + jnp.where(hit, weights_ref[k:k + 1, :], 0.0)
    before = lax.broadcasted_iota(jnp.int32, (tokens, tokens), 0) < lax.broadcasted_iota(jnp.int32, (tokens, tokens), 1)
    position = jnp.dot(
        chosen.astype(jnp.bfloat16), jnp.where(before, 1.0, 0.0).astype(jnp.bfloat16), preferred_element_type=jnp.float32
    )
    slot = (row & (CAP - 1)).astype(jnp.float32)
    select = jnp.where(position == slot, chosen, 0.0)
    combine = select * weight
    high = combine.astype(jnp.bfloat16)
    mix_ref[:slots] = high
    mix_ref[slots:] = (combine - high.astype(jnp.float32)).astype(jnp.bfloat16)
    select = select.astype(jnp.bfloat16)
    copies[2].wait()
    half, width = kept_ref.shape
    tile = 1024
    for start in range(0, width, tile):
        picked = jnp.dot(select, tokens_ref[:, start:start + tile], preferred_element_type=jnp.float32)
        kept_ref[:, start:start + tile] = picked[:half].astype(jnp.bfloat16)
        sent_ref[:, start:start + tile] = picked[half:].astype(jnp.bfloat16)


def route(tokens, expert_ids, gate_weights, chips):
    vmem = pl.BlockSpec(memory_space=pltpu.VMEM)
    count, width = tokens.shape
    half = chips * CAP
    arrays = (expert_ids.T, gate_weights.T, tokens)
    return pl.pallas_call(
        functools.partial(route_kernel, chips),
        out_shape=[
            jax.ShapeDtypeStruct((half, width), jnp.bfloat16),
            jax.ShapeDtypeStruct((half, width), jnp.bfloat16),
            jax.ShapeDtypeStruct((2 * CORES * half, count), jnp.bfloat16),
        ],
        in_specs=[pl.BlockSpec(memory_space=pltpu.HBM)] * 3,
        out_specs=[vmem] * 3,
        scratch_shapes=[pltpu.VMEM(array.shape, array.dtype) for array in arrays] + [pltpu.SemaphoreType.DMA((3,))],
        compiler_params=pltpu.CompilerParams(vmem_limit_bytes=8 * 1024 * 1024),
        cost_estimate=pl.CostEstimate(
            flops=4 * half * CORES * count * width, bytes_accessed=4 * count * width, transcendentals=0
        ),
    )(*[pltpu.with_memory_space_constraint(array, pltpu.HBM) for array in arrays])


PIECES = 4
STEPS = 4


def hold_kernel(source, target, sems):
    rows = source.shape[1] // PIECES
    copies = []
    for piece in range(PIECES):
        at = pl.ds(piece * rows, rows)
        copies.append(pltpu.make_async_copy(source.at[:, at], target.at[:, at], sems.at[piece]))
    for copy in copies:
        copy.start()
    for copy in copies:
        copy.wait()


def hold(weight):
    return pl.pallas_call(
        hold_kernel,
        out_shape=pltpu.VMEM(weight.shape, weight.dtype),
        in_specs=[pl.BlockSpec(memory_space=pltpu.HBM)],
        out_specs=pl.BlockSpec(memory_space=pltpu.VMEM),
        scratch_shapes=[pltpu.SemaphoreType.DMA((PIECES,))],
        compiler_params=pltpu.CompilerParams(vmem_limit_bytes=1024 * 1024),
        cost_estimate=pl.CostEstimate(flops=0, bytes_accessed=4 * weight.size, transcendentals=0),
    )(pltpu.with_memory_space_constraint(weight, pltpu.HBM))


def ffn_kernel(rows_ref, gate_ref, up_ref, down_ref, *out_refs):
    rows = rows_ref[...]
    gate = jnp.dot(rows, gate_ref[0], preferred_element_type=jnp.float32)
    up = jnp.dot(rows, up_ref[0], preferred_element_type=jnp.float32)
    hidden = (gate / (1.0 + jnp.exp(-gate)) * up).astype(jnp.bfloat16)
    part, width = out_refs[0].shape
    tile = 1024
    for start in range(0, width, tile):
        product = jnp.dot(hidden, down_ref[0, :, start:start + tile], preferred_element_type=jnp.float32)
        for i, out_ref in enumerate(out_refs):
            out_ref[:, start:start + tile] = product[i * part:(i + 1) * part].astype(out_ref.dtype)


def ffn(rows, weights, part):
    vmem = pl.BlockSpec(memory_space=pltpu.VMEM)
    units, width = weights[2].shape[1:]
    return pl.pallas_call(
        ffn_kernel,
        out_shape=[jax.ShapeDtypeStruct((part, width), jnp.bfloat16)] * (rows.shape[0] // part),
        in_specs=[vmem] * 4,
        out_specs=[vmem] * (rows.shape[0] // part),
        compiler_params=pltpu.CompilerParams(vmem_limit_bytes=8 * 1024 * 1024),
        cost_estimate=pl.CostEstimate(
            flops=6 * rows.shape[0] * width * units,
            bytes_accessed=2 * width * units,
            transcendentals=rows.shape[0] * units,
        ),
    )(rows, *weights)


def combine_kernel(mix_ref, mine_ref, other_ref, out_hbm, out_ref, sems):
    mix = mix_ref[...].astype(jnp.float32)
    weight = mix.T.astype(jnp.bfloat16)
    width = out_ref.shape[1]
    tile = 1024
    copies = []
    for i, start in enumerate(range(0, width, tile)):
        rows = jnp.concatenate(
            [ref[:, start:start + tile].astype(jnp.float32) for ref in (mine_ref, other_ref)] * 2, axis=0
        ).astype(jnp.bfloat16)
        out_ref[:, start:start + tile] = jnp.dot(
            weight, rows, preferred_element_type=jnp.float32
        ).astype(out_ref.dtype)
        at = pl.ds(start, tile)
        copies.append(pltpu.make_async_copy(out_ref.at[:, at], out_hbm.at[:, at], sems.at[i]))
        copies[-1].start()
    for copy in copies:
        copy.wait()


def combine(mix, mine, other):
    vmem = pl.BlockSpec(memory_space=pltpu.VMEM)
    shape = (mix.shape[1], mine.shape[1])
    return pl.pallas_call(
        combine_kernel,
        out_shape=jax.ShapeDtypeStruct(shape, jnp.bfloat16),
        in_specs=[vmem] * 3,
        out_specs=pl.BlockSpec(memory_space=pltpu.HBM),
        scratch_shapes=[pltpu.VMEM(shape, jnp.bfloat16), pltpu.SemaphoreType.DMA((shape[1] // 1024,))],
        compiler_params=pltpu.CompilerParams(vmem_limit_bytes=8 * 1024 * 1024),
        cost_estimate=pl.CostEstimate(
            flops=2 * mix.shape[0] * shape[0] * shape[1], bytes_accessed=2 * shape[0] * shape[1], transcendentals=0
        ),
    )(mix, mine, other)


def local(tokens, expert_ids, gate_weights, w_gate, w_up, w_down):
    window = lax.axis_size("expert")
    shards = lax.axis_size("dp")
    chips = window // CORES
    width = tokens.shape[1]
    kept, sent, mix = route(tokens, expert_ids, gate_weights, chips)

    core_pairs = [(i, i ^ 1) for i in range(window)]

    def travel(block, chip_shift, dp_bit):
        pairs = []
        for c in range(chips):
            for k in range(CORES):
                for z in range(shards):
                    to_chip = (c + chip_shift) % chips
                    pairs.append(((c * CORES + k) * shards + z, (to_chip * CORES + k) * shards + (z ^ dp_bit)))
        return lax.ppermute(block, ("expert", "dp"), pairs)

    bits = [1 << i for i in range((shards - 1).bit_length())]

    half = chips * CAP
    swapped = lax.ppermute(sent, "expert", core_pairs).reshape(chips, CAP, width)
    blocks = jnp.concatenate([kept.reshape(chips, CAP, width), swapped], axis=1)
    size = CORES * CAP
    held = {0: blocks.reshape(chips * size, width)}
    for bit in reversed(bits[1:]):
        for offset in list(held):
            held[offset ^ bit] = [travel(held[offset][x * size:(x + 1) * size], 0, bit) for x in range(chips)]
            held[offset ^ bit] = jnp.concatenate(held[offset ^ bit], axis=0)
    early, late = {}, {}
    for offset in list(held):
        for x in range(chips):
            block = held[offset][x * size:(x + 1) * size]
            for bit in [0] + bits[:1]:
                arrived = travel(block, x, bit) if x or bit else block
                (late if offset and (x or bit) else early)[x, offset ^ bit] = arrived

    w_up, _ = lax.optimization_barrier((w_up, swapped))
    weights = [pltpu.with_memory_space_constraint(w, pltpu.VMEM) for w in (w_gate, hold(w_up), w_down)]
    parts = {}
    for some in (early, late):
        blocks = list(some.values())
        if parts:
            blocks, _ = lax.optimization_barrier((blocks, parts[0, 0]))
        if some:
            parts.update(zip(some, ffn(jnp.concatenate(blocks, axis=0), weights, size)))

    home = {x: [] for x in range(chips)}
    relayed = []
    last = [(x, 0, 0) for x in range(chips)]
    for bit in bits:
        for x in reversed(range(chips)):
            for offset in [o for o in reversed(range(shards)) if (x, o) in parts and o & bit]:
                if offset == bit:
                    last.append((x, offset, bit))
                else:
                    arrived = travel(parts.pop((x, offset)), 0, bit)
                    onward = (x, offset ^ bit)
                    parts[onward] = (parts[onward].astype(jnp.float32) + arrived.astype(jnp.float32)).astype(jnp.bfloat16)
                    relayed.append(arrived)
    plain = [(x, offset) for x, offset, bit in last if offset <= 1 and relayed and (x or offset)]
    waited, _ = lax.optimization_barrier(([parts[way] for way in plain], relayed))
    parts.update(zip(plain, waited))
    for x, offset, bit in last:
        shift = (chips - x) % chips
        block = parts[x, offset]
        home[x].append(travel(block, shift, bit) if shift or bit else block)
    home = jnp.stack([sum(block.astype(jnp.float32) for block in home[x]).astype(jnp.bfloat16) for x in range(chips)])
    mine = home[:, :CAP].reshape(half, width)
    other = lax.ppermute(home[:, CAP:].reshape(half, width), "expert", core_pairs)
    return combine(mix, mine, other)


def solution(mesh):
    placed = (
        P(("groups", "expert", "dp"), None),
        P(("groups", "expert", "dp"), None),
        P(("groups", "expert", "dp"), None),
        P("expert", None, "dp"),
        P("expert", None, "dp"),
        P("expert", "dp", None),
    )
    return jax.shard_map(
        local,
        mesh=mesh,
        in_specs=placed,
        out_specs=P(("groups", "expert", "dp"), None),
        check_vma=False,
    )
```

```python
import functools

import jax
import jax.numpy as jnp
from jax import lax
from jax.experimental import pallas as pl
from jax.experimental.pallas import tpu as pltpu
from jax.sharding import PartitionSpec as P

CAP = 4
CORES = 2


def route_kernel(chips, *refs):
    sources, (kept_ref, sent_ref, mix_ref), (ids_ref, weights_ref, tokens_ref, sems) = refs[:3], refs[3:6], refs[6:]
    copies = [
        pltpu.make_async_copy(source, target, sems.at[i])
        for i, (source, target) in enumerate(zip(sources, (ids_ref, weights_ref, tokens_ref)))
    ]
    for copy in copies:
        copy.start()
    me = lax.axis_index("expert")
    chip, core = me // CORES, me % CORES
    slots = CORES * chips * CAP
    topk, tokens = ids_ref.shape
    row = lax.broadcasted_iota(jnp.int32, (slots, tokens), 0)
    expert = jnp.zeros_like(row)
    for i in range(CORES * chips):
        core_offset, chip_offset = i // chips, i % chips
        named = lax.rem(chip + chip_offset, chips) * CORES + lax.rem(core + core_offset, CORES)
        expert = jnp.where((row >= i * CAP) & (row < (i + 1) * CAP), named, expert)
    copies[0].wait()
    copies[1].wait()
    chosen = jnp.zeros((slots, tokens), jnp.float32)
    weight = jnp.zeros((slots, tokens), jnp.float32)
    for k in range(topk):
        hit = ids_ref[k:k + 1, :] == expert
        chosen = jnp.where(hit, 1.0, chosen)
        weight = weight + jnp.where(hit, weights_ref[k:k + 1, :], 0.0)
    before = lax.broadcasted_iota(jnp.int32, (tokens, tokens), 0) < lax.broadcasted_iota(jnp.int32, (tokens, tokens), 1)
    position = jnp.dot(
        chosen.astype(jnp.bfloat16), jnp.where(before, 1.0, 0.0).astype(jnp.bfloat16), preferred_element_type=jnp.float32
    )
    slot = (row & (CAP - 1)).astype(jnp.float32)
    select = jnp.where(position == slot, chosen, 0.0)
    combine = select * weight
    high = combine.astype(jnp.bfloat16)
    mix_ref[:slots] = high
    mix_ref[slots:] = (combine - high.astype(jnp.float32)).astype(jnp.bfloat16)
    select = select.astype(jnp.bfloat16)
    copies[2].wait()
    half, width = kept_ref.shape
    tile = 1024
    for start in range(0, width, tile):
        picked = jnp.dot(select, tokens_ref[:, start:start + tile], preferred_element_type=jnp.float32)
        kept_ref[:, start:start + tile] = picked[:half].astype(jnp.bfloat16)
        sent_ref[:, start:start + tile] = picked[half:].astype(jnp.bfloat16)


def route(tokens, expert_ids, gate_weights, chips):
    vmem = pl.BlockSpec(memory_space=pltpu.VMEM)
    count, width = tokens.shape
    half = chips * CAP
    arrays = (expert_ids.T, gate_weights.T, tokens)
    return pl.pallas_call(
        functools.partial(route_kernel, chips),
        out_shape=[
            jax.ShapeDtypeStruct((half, width), jnp.bfloat16),
            jax.ShapeDtypeStruct((half, width), jnp.bfloat16),
            jax.ShapeDtypeStruct((2 * CORES * half, count), jnp.bfloat16),
        ],
        in_specs=[pl.BlockSpec(memory_space=pltpu.HBM)] * 3,
        out_specs=[vmem] * 3,
        scratch_shapes=[pltpu.VMEM(array.shape, array.dtype) for array in arrays] + [pltpu.SemaphoreType.DMA((3,))],
        compiler_params=pltpu.CompilerParams(vmem_limit_bytes=8 * 1024 * 1024),
        cost_estimate=pl.CostEstimate(
            flops=4 * half * CORES * count * width, bytes_accessed=4 * count * width, transcendentals=0
        ),
    )(*[pltpu.with_memory_space_constraint(array, pltpu.HBM) for array in arrays])


PIECES = 4
STEPS = 4


def hold_kernel(source, target, sems):
    rows = source.shape[1] // PIECES
    copies = []
    for piece in range(PIECES):
        at = pl.ds(piece * rows, rows)
        copies.append(pltpu.make_async_copy(source.at[:, at], target.at[:, at], sems.at[piece]))
    for copy in copies:
        copy.start()
    for copy in copies:
        copy.wait()


def hold(weight):
    return pl.pallas_call(
        hold_kernel,
        out_shape=pltpu.VMEM(weight.shape, weight.dtype),
        in_specs=[pl.BlockSpec(memory_space=pltpu.HBM)],
        out_specs=pl.BlockSpec(memory_space=pltpu.VMEM),
        scratch_shapes=[pltpu.SemaphoreType.DMA((PIECES,))],
        compiler_params=pltpu.CompilerParams(vmem_limit_bytes=1024 * 1024),
        cost_estimate=pl.CostEstimate(flops=0, bytes_accessed=4 * weight.size, transcendentals=0),
    )(pltpu.with_memory_space_constraint(weight, pltpu.HBM))


def ffn_kernel(rows_ref, gate_ref, up_ref, down_ref, *out_refs):
    rows = rows_ref[...]
    gate = jnp.dot(rows, gate_ref[0], preferred_element_type=jnp.float32)
    up = jnp.dot(rows, up_ref[0], preferred_element_type=jnp.float32)
    hidden = (gate / (1.0 + jnp.exp(-gate)) * up).astype(jnp.bfloat16)
    part, width = out_refs[0].shape
    tile = 1024
    for start in range(0, width, tile):
        product = jnp.dot(hidden, down_ref[0, :, start:start + tile], preferred_element_type=jnp.float32)
        for i, out_ref in enumerate(out_refs):
            out_ref[:, start:start + tile] = product[i * part:(i + 1) * part].astype(out_ref.dtype)


def ffn(rows, weights, part):
    vmem = pl.BlockSpec(memory_space=pltpu.VMEM)
    units, width = weights[2].shape[1:]
    return pl.pallas_call(
        ffn_kernel,
        out_shape=[jax.ShapeDtypeStruct((part, width), jnp.bfloat16)] * (rows.shape[0] // part),
        in_specs=[vmem] * 4,
        out_specs=[vmem] * (rows.shape[0] // part),
        compiler_params=pltpu.CompilerParams(vmem_limit_bytes=8 * 1024 * 1024),
        cost_estimate=pl.CostEstimate(
            flops=6 * rows.shape[0] * width * units,
            bytes_accessed=2 * width * units,
            transcendentals=rows.shape[0] * units,
        ),
    )(rows, *weights)


def combine_kernel(mix_ref, mine_ref, other_ref, out_hbm, out_ref, sems):
    mix = mix_ref[...].astype(jnp.float32)
    weight = mix.T.astype(jnp.bfloat16)
    width = out_ref.shape[1]
    tile = 1024
    copies = []
    for i, start in enumerate(range(0, width, tile)):
        rows = jnp.concatenate(
            [ref[:, start:start + tile].astype(jnp.float32) for ref in (mine_ref, other_ref)] * 2, axis=0
        ).astype(jnp.bfloat16)
        out_ref[:, start:start + tile] = jnp.dot(
            weight, rows, preferred_element_type=jnp.float32
        ).astype(out_ref.dtype)
        at = pl.ds(start, tile)
        copies.append(pltpu.make_async_copy(out_ref.at[:, at], out_hbm.at[:, at], sems.at[i]))
        copies[-1].start()
    for copy in copies:
        copy.wait()


def combine(mix, mine, other):
    vmem = pl.BlockSpec(memory_space=pltpu.VMEM)
    shape = (mix.shape[1], mine.shape[1])
    return pl.pallas_call(
        combine_kernel,
        out_shape=jax.ShapeDtypeStruct(shape, jnp.bfloat16),
        in_specs=[vmem] * 3,
        out_specs=pl.BlockSpec(memory_space=pltpu.HBM),
        scratch_shapes=[pltpu.VMEM(shape, jnp.bfloat16), pltpu.SemaphoreType.DMA((shape[1] // 1024,))],
        compiler_params=pltpu.CompilerParams(vmem_limit_bytes=8 * 1024 * 1024),
        cost_estimate=pl.CostEstimate(
            flops=2 * mix.shape[0] * shape[0] * shape[1], bytes_accessed=2 * shape[0] * shape[1], transcendentals=0
        ),
    )(mix, mine, other)


def local(tokens, expert_ids, gate_weights, w_gate, w_up, w_down):
    window = lax.axis_size("expert")
    shards = lax.axis_size("dp")
    chips = window // CORES
    width = tokens.shape[1]
    kept, sent, mix = route(tokens, expert_ids, gate_weights, chips)

    core_pairs = [(i, i ^ 1) for i in range(window)]

    def travel(block, chip_shift, dp_bit):
        pairs = []
        for c in range(chips):
            for k in range(CORES):
                for z in range(shards):
                    to_chip = (c + chip_shift) % chips
                    pairs.append(((c * CORES + k) * shards + z, (to_chip * CORES + k) * shards + (z ^ dp_bit)))
        return lax.ppermute(block, ("expert", "dp"), pairs)

    bits = [1 << i for i in range((shards - 1).bit_length())]

    half = chips * CAP
    swapped = lax.ppermute(sent, "expert", core_pairs).reshape(chips, CAP, width)
    blocks = jnp.concatenate([kept.reshape(chips, CAP, width), swapped], axis=1)
    size = CORES * CAP
    held = {0: blocks.reshape(chips * size, width)}
    early, late = {(0, 0): blocks[0]}, {}
    for x, bit in [(x, bit) for x in range(chips) for bit in reversed([0] + bits[:1])]:
        if x or bit:
            early[x, bit] = travel(blocks[x], x, bit)
    for bit in reversed(bits[1:]):
        for offset in list(held):
            held[offset ^ bit] = [travel(held[offset][x * size:(x + 1) * size], 0, bit) for x in range(chips)]
            held[offset ^ bit] = jnp.concatenate(held[offset ^ bit], axis=0)
    for offset in list(held):
        if offset:
            for x in range(chips):
                block = held[offset][x * size:(x + 1) * size]
                for bit in [0] + bits[:1]:
                    arrived = travel(block, x, bit) if x or bit else block
                    (late if x or bit else early)[x, offset ^ bit] = arrived

    w_up, _ = lax.optimization_barrier((w_up, swapped))
    weights = [pltpu.with_memory_space_constraint(w, pltpu.VMEM) for w in (w_gate, hold(w_up), w_down)]
    parts = {}
    for some in (early, late):
        blocks = list(some.values())
        if parts:
            blocks, _ = lax.optimization_barrier((blocks, parts[0, 0]))
        if some:
            parts.update(zip(some, ffn(jnp.concatenate(blocks, axis=0), weights, size)))

    home = {x: [] for x in range(chips)}
    relayed = []
    last = [(x, 0, 0) for x in range(chips)]
    for bit in bits:
        for x in reversed(range(chips)):
            for offset in [o for o in reversed(range(shards)) if (x, o) in parts and o & bit]:
                if offset == bit:
                    last.append((x, offset, bit))
                else:
                    arrived = travel(parts.pop((x, offset)), 0, bit)
                    onward = (x, offset ^ bit)
                    parts[onward] = (parts[onward].astype(jnp.float32) + arrived.astype(jnp.float32)).astype(jnp.bfloat16)
                    relayed.append(arrived)
    plain = [(x, offset) for x, offset, bit in last if offset == 1 and relayed]
    waited, _ = lax.optimization_barrier(([parts[way] for way in plain], relayed))
    parts.update(zip(plain, waited))
    for x, offset, bit in last:
        shift = (chips - x) % chips
        block = parts[x, offset]
        home[x].append(travel(block, shift, bit) if shift or bit else block)
    home = jnp.stack([sum(block.astype(jnp.float32) for block in home[x]).astype(jnp.bfloat16) for x in range(chips)])
    mine = home[:, :CAP].reshape(half, width)
    other = lax.ppermute(home[:, CAP:].reshape(half, width), "expert", core_pairs)
    return combine(mix, mine, other)


def solution(mesh):
    placed = (
        P(("groups", "expert", "dp"), None),
        P(("groups", "expert", "dp"), None),
        P(("groups", "expert", "dp"), None),
        P("expert", None, "dp"),
        P("expert", None, "dp"),
        P("expert", "dp", None),
    )
    return jax.shard_map(
        local,
        mesh=mesh,
        in_specs=placed,
        out_specs=P(("groups", "expert", "dp"), None),
        check_vma=False,
    )
```
